32 devices in a mesh: row: 4 (over y, x), col: 8 (over z, core).
Axes of the slice: x: 2, y: 2, z: 4, core: 2. Of those that a mesh axis runs over, the one named last changes fastest.
Arguments:
- tokens: bfloat16 [1024, 2304], P('row', 'col'), may hold values from -6 to 6
- gate_weight: bfloat16 [8, 2304, 5760], P(None, 'col', 'row'), may hold values from -0.125 to 0.125
- up_weight: bfloat16 [8, 2304, 5760], P(None, 'col', 'row'), may hold values from -0.125 to 0.125
- down_weight: bfloat16 [8, 5760, 2304], P(None, 'row', 'col'), may hold values from -0.078125 to 0.078125
- route_ids: int32 [1024, 2], replicated, may hold values from 0 to 7, all different within a row; in each aligned block of 1024 rows (0 to 1023, 1024 to 2047, ...) at most 512 rows name the same one
- route_weight: float32 [1024, 2], replicated, may hold values from 0.2 to 1
- prefill_cache: bfloat16 [2, 256, 16, 2304], P(None, ('row', 'col')), may hold values from -6 to 6
- dest_col: int32 [4, 8, 8], P('row'), may hold values from 0 to 7, as said below
- dest_slot: int32 [4, 8, 8], P('row'), may hold values from 0 to 7, as said below
- pages_used: int32 [4, 8], P('row'), may hold values from 2 to 8, as said below
Outputs:
- mixed: bfloat16 [1024, 2304], P('row', 'col')
- decode_cache: bfloat16 [2, 256, 16, 2304], P(None, ('row', 'col'))
The draws below stay inside these ranges and needn't reach their ends.
Inputs may be any that keep to these rules, and one draw needn't show every extreme that they name: `route_ids`: each token names two different experts; no expert is named by more than 512 tokens, a bound that some block reaches. For every device (r, c), dest_col[r, c, :] names each col index exactly 1 times. For every r and col index c2, the page slots of row r with dest_col = c2 carry distinct dest_slot values, so they fill all 8 slots of device (r, c2). The live slots of a device are its first pages_used slots; some device has all 8 live.
All inputs are finite; a program needn't handle non-finite values.
Results may differ from the reference program's by a relative error of at most 0.03.
Values may be sent and summed in bfloat16 or wider, within the bound.
A program may use at most 192 MiB of HBM per device.

```python
import math
import jax
import jax.numpy as jnp
import numpy as np
from jax import lax

D = 2304
FF = 5760
EXPERTS = 8
HEADS = 36
HEAD_DIM = 64
PAGE = 16
PEER = 1
TOKENS = 1024
CAP = 512
SLOTS = 8
N_ROW = 4
N_COL = 8


def one_permutation(sub_key):
    return jax.random.permutation(sub_key, SLOTS).astype(jnp.int32)


def page_plan(key):
    device_count = N_ROW * N_COL
    send_keys = jax.random.split(jax.random.fold_in(key, 11), device_count)
    recv_keys = jax.random.split(jax.random.fold_in(key, 23), device_count)
    send_perm = jax.vmap(one_permutation)(send_keys).reshape(N_ROW, N_COL, SLOTS)
    recv_perm = jax.vmap(one_permutation)(recv_keys).reshape(N_ROW, N_COL, SLOTS)
    dest_index = send_perm // PEER
    arrival = jnp.arange(N_COL, dtype=jnp.int32)[None, :, None] * PEER + send_perm % PEER
    row_index = jnp.arange(N_ROW, dtype=jnp.int32)[:, None, None]
    slot_table = recv_perm[row_index, dest_index, arrival]
    return (dest_index.astype(jnp.int32), slot_table.astype(jnp.int32))


def draw_dest_col(key, part):
    return page_plan(key)[0]


def draw_dest_slot(key, part):
    return page_plan(key)[1]


def draw_pages_used(key, part):
    keys = jax.random.split(jax.random.fold_in(key, 37), 3)
    halving = jax.random.randint(keys[0], (N_ROW, N_COL), 0, 3)
    base_count = jnp.right_shift(jnp.full((N_ROW, N_COL), SLOTS, jnp.int32), halving)
    extra_count = jax.random.randint(keys[1], (N_ROW, N_COL), 0, SLOTS // 8 + 1)
    used_count = jnp.minimum(base_count + extra_count, SLOTS).reshape(-1)
    full_device = jax.random.randint(keys[2], (), 0, N_ROW * N_COL)
    used_count = jnp.where(jnp.arange(N_ROW * N_COL) == full_device, SLOTS, used_count)
    return used_count.reshape(N_ROW, N_COL).astype(jnp.int32)


def block_scale(key, shape, cuts, smallest, high):
    level, own = 1.0, jax.random.fold_in(key, 6)
    for axis_at, blocks in cuts:
        draws = jnp.exp(jax.random.uniform(jax.random.fold_in(own, axis_at), (blocks,), jnp.float32, smallest / len(cuts), high / len(cuts)))
        level = level * jnp.repeat(draws, shape[axis_at] // blocks).reshape([-1 if axis == axis_at else 1 for axis in range(len(shape))])
    return level


def deal_out(stream_key, own, number, rows, amount, top, most, skew):
    sequence = jax.random.permutation(stream_key, amount)
    heavy_load, usual = shares(amount, rows * top, most, skew, True), shares(amount, rows * top, most, skew, False)
    places = jnp.arange(amount)

    def named(tallies, turn):
        used = int((tallies > 0).sum())
        fixed = max(1, used // 4)
        passed = fixed + (places - fixed + turn * (used - fixed)) % max(1, amount - fixed)
        return jnp.zeros((amount,), jnp.int32).at[sequence[jnp.where(places < fixed, places, passed)]].set(jnp.asarray(tallies, jnp.int32))

    tallies = jnp.where(number % 4 == 0, named(heavy_load, number // 4), named(usual, number - number // 4 - 1))
    mixed = jax.random.permutation(jax.random.fold_in(own, 3), amount)
    source_of, taker = mixed[0:amount // 2 * 2:2], mixed[1:amount // 2 * 2:2]
    margin = jnp.minimum(tallies[source_of] - 1, most - tallies[taker]) // 2
    margin = jnp.where((source_of == sequence[0]) | (taker == sequence[0]) | (tallies[taker] == 0), 0, jnp.maximum(margin, 0))
    passed = jax.random.randint(jax.random.fold_in(own, 4), (amount // 2,), 0, 1 << 20) % (margin + 1)
    tallies = tallies.at[source_of].add(-passed).at[taker].add(passed)
    members = jnp.searchsorted(jnp.cumsum(tallies), jnp.arange(rows * top), side="right").astype(jnp.int32)
    listing = members.reshape(top, rows).T
    listing = listing[jax.random.permutation(jax.random.fold_in(own, 1), rows)]
    turn = jax.random.randint(jax.random.fold_in(own, 2), (rows, 1), 0, top)
    return jnp.take_along_axis(listing, (jnp.arange(top)[None, :] + turn) % top, axis=1)


def shares(count, total, limit, skew, full):
    loads = [(1 << 20) // math.isqrt(standing ** skew) + 1 for standing in range(1, count + 1)]
    largest = limit if full else min(limit, max(-(-total // count), total * loads[0] // sum(loads)))
    least = 1 if total - largest >= count - 1 else 0
    holding, spare = [largest] + [least] * (count - 1), total - largest - least * (count - 1)
    while spare > 0:
        movable = [i for i in range(1, count) if holding[i] < largest] or [i for i in range(1, count) if holding[i] < limit]
        mass, left = sum([loads[i] for i in movable]), spare
        for i in movable:
            addition = min(limit - holding[i], max(1, left * loads[i] // mass), spare)
            holding[i] = holding[i] + addition
            spare = spare - addition
    return np.array(holding)


def scatter_about(key, dims, scale, bound, cuts=(), held_as=jnp.bfloat16):
    entries = scale * jax.random.normal(key, dims, jnp.float32)
    if cuts:
        entries = entries * block_scale(key, dims, cuts, -0.22, 0.18)
    return jnp.clip(entries, -bound, bound).astype(held_as)


def setup_inputs(seed: int = 0) -> dict:
    splits = jax.random.split(jax.random.key(seed), 11)
    tokens = scatter_about(splits[0], (TOKENS, D), 1.0, 6.0, ((0, 4), (1, 8)))
    gate_weight = scatter_about(splits[1], (EXPERTS, D, FF), D ** -0.5, 0.125, ((1, 8), (2, 4)))
    up_weight = scatter_about(splits[2], (EXPERTS, D, FF), D ** -0.5, 0.125, ((1, 8), (2, 4)))
    down_weight = scatter_about(splits[3], (EXPERTS, FF, D), FF ** -0.5, 0.078125, ((1, 4), (2, 8)))
    route_ids_keys = jax.random.split(jax.random.fold_in(splits[4], 1), TOKENS // TOKENS)
    route_ids_turns = jax.random.permutation(jax.random.fold_in(splits[4], 3), TOKENS // TOKENS)
    route_ids = jax.vmap(lambda own, number: deal_out(jax.random.fold_in(splits[4], 2), own, number, TOKENS, EXPERTS, 2, CAP, 1))(route_ids_keys, route_ids_turns).reshape((TOKENS, 2))
    route_weight = jnp.clip(jax.random.uniform(splits[5], (TOKENS, 2), jnp.float32, 0.2, 1.0), 0.2, 1.0)
    prefill_cache = scatter_about(splits[6], (2, N_ROW * N_COL * SLOTS, PAGE, HEADS * HEAD_DIM), 1.0, 6.0, ((1, 32),))
    dest_col = draw_dest_col(jax.random.fold_in(splits[10], 71), 0)
    dest_slot = draw_dest_slot(jax.random.fold_in(splits[10], 71), 0)
    pages_used = draw_pages_used(jax.random.fold_in(splits[10], 71), 0)
    return dict(tokens=tokens, gate_weight=gate_weight, up_weight=up_weight, down_weight=down_weight, route_ids=route_ids, route_weight=route_weight, prefill_cache=prefill_cache, dest_col=dest_col, dest_slot=dest_slot, pages_used=pages_used)


def expert_order(route_ids):
    flat_expert = route_ids.reshape(-1).astype(jnp.int32)
    sort_order = jnp.argsort(flat_expert, stable=True).astype(jnp.int32)
    labels = jnp.arange(EXPERTS, dtype=jnp.int32)
    below = jnp.sum((flat_expert[None, :] < labels[:, None]).astype(jnp.int32), axis=1)
    starts = jnp.minimum(below, flat_expert.shape[0] - CAP)
    return sort_order, flat_expert[sort_order], starts


def reference(tokens, gate_weight, up_weight, down_weight, route_ids, route_weight, prefill_cache, dest_col, dest_slot, pages_used):
    sort_order, row_expert, starts = expert_order(route_ids)
    row_token = sort_order // 2
    slot_rows = tokens[row_token]
    row_weight = route_weight.reshape(-1)[sort_order]
    assignments = slot_rows.shape[0]
    block_width = D // N_COL
    totals = jnp.zeros((assignments, D), jnp.float32)
    for expert in range(EXPERTS):
        window_start = starts[expert]
        window = lax.dynamic_slice_in_dim(slot_rows, window_start, CAP, 0)
        paired = jnp.concatenate([gate_weight[expert], up_weight[expert]], axis=1)
        summed = jnp.zeros((CAP, 2 * FF), jnp.float32)
        for block_index in range(N_COL):
            lower = block_index * block_width
            upper = lower + block_width
            part_sum = jnp.dot(window[:, lower:upper], paired[lower:upper], preferred_element_type=jnp.float32)
            rounded = lax.optimization_barrier(part_sum.astype(jnp.bfloat16))
            summed = summed + rounded.astype(jnp.float32)
        gate_part = summed[:, :FF]
        up_part = summed[:, FF:]
        weight_window = lax.dynamic_slice_in_dim(row_weight, window_start, CAP, 0)
        hidden = (weight_window[:, None] * jax.nn.silu(gate_part) * up_part).astype(jnp.bfloat16)
        down_rows = jnp.dot(hidden, down_weight[expert], preferred_element_type=jnp.float32)
        is_owner = lax.dynamic_slice_in_dim(row_expert, window_start, CAP, 0) == expert
        current = lax.dynamic_slice_in_dim(totals, window_start, CAP, 0)
        totals = lax.dynamic_update_slice_in_dim(totals, jnp.where(is_owner[:, None], down_rows, current), window_start, 0)
    mixed = jnp.zeros((TOKENS, D), jnp.float32).at[row_token].add(totals).astype(jnp.bfloat16)

    cache_width = prefill_cache.shape[3]
    page_index = jnp.arange(SLOTS, dtype=jnp.int32)
    is_live = page_index[None, None, :] < pages_used[:, :, None]
    source_pages = prefill_cache.reshape(2, N_ROW, N_COL, SLOTS, PAGE, cache_width)
    masked = jnp.where(is_live[None, :, :, :, None, None], source_pages, jnp.zeros((), prefill_cache.dtype))
    masked = masked.reshape(prefill_cache.shape)
    row_base = jnp.arange(N_ROW, dtype=jnp.int32)[:, None, None] * N_COL
    target = ((row_base + dest_col) * SLOTS + dest_slot).reshape(-1).astype(jnp.int32)
    decode_cache = jnp.zeros_like(prefill_cache).at[:, target].set(masked)
    return mixed, decode_cache
```

```python
import jax
import jax.numpy as jnp
from jax import lax
from jax.experimental import pallas as pl
from jax.experimental.pallas import tpu as pltpu
from jax.sharding import PartitionSpec as P

TILE = 256
VMEM_BYTES = 48 * 1024 * 1024


def sorted_places(route_ids, experts):
    tokens = route_ids.shape[0]
    group = 128
    labels = jnp.arange(experts, dtype=jnp.int32)
    onehot = (route_ids[:, :, None] == labels).astype(jnp.float32)
    per_token = jnp.sum(onehot, axis=1).reshape(tokens // group, group, experts)
    below = jnp.tril(jnp.ones((group, group), jnp.bfloat16), -1)
    within = jnp.einsum(
        "ij,bje->bie", below, per_token.astype(jnp.bfloat16), preferred_element_type=jnp.float32
    )
    totals = jnp.sum(per_token, axis=1)
    blocks = jnp.arange(tokens // group)
    earlier = jnp.sum(jnp.where(blocks[:, None, None] > blocks[None, :, None], totals[None], 0.0), axis=1)
    counts = jnp.sum(totals, axis=0)
    starts = jnp.sum(jnp.where(labels[:, None] > labels[None, :], counts[None, :], 0.0), axis=1)
    base = (within + earlier[:, None, :] + starts).reshape(tokens, experts)
    places = jnp.sum(onehot * base[:, None, :], axis=2).astype(jnp.int32)
    starts = starts.astype(jnp.int32)
    return places, starts, starts + counts.astype(jnp.int32)


def step_table(starts, ends, rows):
    experts = starts.shape[0]
    tiles = rows // TILE
    labels = jnp.arange(experts, dtype=jnp.int32)
    spans = jnp.where(ends > starts, (ends - 1) // TILE - starts // TILE + 1, 0)
    after = jnp.sum(jnp.where(labels[:, None] >= labels[None, :], spans[None, :], 0), axis=1)
    step = jnp.arange(tiles + experts - 1, dtype=jnp.int32)
    expert = jnp.minimum(jnp.sum((after[None, :] <= step[:, None]).astype(jnp.int32), axis=1), experts - 1)
    chosen = expert[:, None] == labels[None, :]

    def pick(table):
        return jnp.sum(jnp.where(chosen, table[None, :], 0), axis=1)

    live = step < after[experts - 1]
    tile = jnp.where(live, pick(starts) // TILE + step - pick(after - spans), tiles - 1)
    low = jnp.where(live, jnp.maximum(pick(starts), tile * TILE), 0)
    high = jnp.where(live, jnp.minimum(pick(ends), tile * TILE + TILE), 0)
    return tile, expert, low, high


def up_kernel(tile, expert, low, high, first, second, tokens, gate, up, out):
    s = pl.program_id(0)
    place = tile[s] * TILE + lax.broadcasted_iota(jnp.int32, (TILE, 1), 0)
    mask = (place >= low[s]) & (place < high[s])
    pick = (first[...] == place) | (second[...] == place)
    rows = jnp.dot(
        jnp.where(pick, 1.0, 0.0).astype(jnp.bfloat16), tokens[...], preferred_element_type=jnp.float32
    ).astype(jnp.bfloat16)
    for i, weight in enumerate((gate, up)):
        product = jnp.dot(rows, weight[0], preferred_element_type=jnp.float32)
        out[i] = jnp.where(mask, product, out[i].astype(jnp.float32)).astype(jnp.bfloat16)


def up_products(table, places, tokens, gate_weight, up_weight):
    count = tokens.shape[0]
    rows = 2 * count
    _, depth, width = gate_weight.shape
    whole = lambda s, *_: (0, 0)
    weight = pl.BlockSpec((1, depth, width), lambda s, tile, expert, *_: (expert[s], 0, 0))
    return pl.pallas_call(
        up_kernel,
        out_shape=jax.ShapeDtypeStruct((2, rows, width), jnp.bfloat16),
        grid_spec=pltpu.PrefetchScalarGridSpec(
            num_scalar_prefetch=4,
            grid=(table[0].shape[0],),
            in_specs=[
                pl.BlockSpec((1, count), whole),
                pl.BlockSpec((1, count), whole),
                pl.BlockSpec((count, depth), whole),
                weight,
                weight,
            ],
            out_specs=pl.BlockSpec((2, TILE, width), lambda s, tile, *_: (0, tile[s], 0)),
        ),
        compiler_params=pltpu.CompilerParams(vmem_limit_bytes=VMEM_BYTES),
    )(*table, places[:, 0].reshape(1, -1), places[:, 1].reshape(1, -1), tokens, gate_weight, up_weight)


def down_kernel(tile, expert, low, high, first, second, hidden, weight, out, total):
    s = pl.program_id(0)

    @pl.when(s == 0)
    def _():
        total[...] = jnp.zeros_like(total)

    place = tile[s] * TILE + lax.broadcasted_iota(jnp.int32, (1, TILE), 1)
    mask = (place >= low[s]) & (place < high[s])
    place = jnp.where(mask, place, -1)
    pick = (first[...] == place) | (second[...] == place)
    product = jnp.dot(hidden[...], weight[0], preferred_element_type=jnp.float32).astype(jnp.bfloat16)
    total[...] += jnp.dot(
        jnp.where(pick, 1.0, 0.0).astype(jnp.bfloat16), product, preferred_element_type=jnp.float32
    )

    @pl.when(s == pl.num_programs(0) - 1)
    def _():
        out[...] = total[...].astype(jnp.bfloat16)


def down_products(table, places, hidden, down_weight):
    count = places.shape[0]
    _, width, depth = down_weight.shape
    whole = lambda s, *_: (0, 0)
    return pl.pallas_call(
        down_kernel,
        out_shape=jax.ShapeDtypeStruct((count, depth), jnp.bfloat16),
        grid_spec=pltpu.PrefetchScalarGridSpec(
            num_scalar_prefetch=4,
            grid=(table[0].shape[0],),
            in_specs=[
                pl.BlockSpec((count, 1), whole),
                pl.BlockSpec((count, 1), whole),
                pl.BlockSpec((TILE, width), lambda s, tile, *_: (tile[s], 0)),
                pl.BlockSpec((1, width, depth), lambda s, tile, expert, *_: (expert[s], 0, 0)),
            ],
            out_specs=pl.BlockSpec((count, depth), whole),
            scratch_shapes=[pltpu.VMEM((count, depth), jnp.float32)],
        ),
        compiler_params=pltpu.CompilerParams(vmem_limit_bytes=VMEM_BYTES),
    )(*table, places[:, 0:1], places[:, 1:2], hidden, down_weight)


def page_kernel(source, keep, page, out):
    live = jnp.broadcast_to(keep[pl.program_id(0)] > 0, out.shape)
    out[...] = jnp.where(live, page[...], jnp.zeros_like(page))


def take_pages(cache, source, keep):
    block = (cache.shape[0], 1, *cache.shape[2:])
    return pl.pallas_call(
        page_kernel,
        out_shape=jax.ShapeDtypeStruct(cache.shape, cache.dtype),
        grid_spec=pltpu.PrefetchScalarGridSpec(
            num_scalar_prefetch=2,
            grid=(source.shape[0],),
            in_specs=[pl.BlockSpec(block, lambda p, source, keep: (0, source[p], 0, 0))],
            out_specs=pl.BlockSpec(block, lambda p, source, keep: (0, p, 0, 0)),
        ),
    )(source, keep, cache)


def move_pages(prefill_cache, dest_col, dest_slot, pages_used):
    col_devices = lax.axis_size("col")
    own = lax.axis_index("col")
    slots = prefill_cache.shape[1]
    per_peer = slots // col_devices
    page = jnp.arange(slots, dtype=jnp.int32)
    peers = jnp.arange(col_devices, dtype=jnp.int32)
    table = dest_col[0]
    earlier = (table[:, :, None] == table[:, None, :]) & (page[None, :] < page[:, None])[None]
    order = jnp.sum(earlier.astype(jnp.int32), axis=2)
    sends = table * per_peer + order
    is_own = (peers == own)[:, None]
    own_sends = jnp.sum(jnp.where(is_own, sends, 0), axis=0)
    own_used = jnp.sum(jnp.where(peers == own, pages_used[0], 0))
    source = jnp.sum(jnp.where(own_sends[None, :] == page[:, None], page[None, :], 0), axis=1)
    received = lax.all_to_all(
        take_pages(prefill_cache, source, (source < own_used).astype(jnp.int32)),
        "col",
        split_axis=1,
        concat_axis=1,
        tiled=True,
    )
    arrival = peers[:, None] * per_peer + order
    mine = (table == own)[None] & (dest_slot[0][None] == page[:, None, None])
    origin = jnp.sum(jnp.where(mine, arrival[None], 0), axis=(1, 2))
    return take_pages(received, origin, jnp.ones_like(origin))


def shards(
    tokens,
    gate_weight,
    up_weight,
    down_weight,
    route_ids,
    route_weight,
    prefill_cache,
    dest_col,
    dest_slot,
    pages_used,
):
    rows = 2 * route_ids.shape[0]
    gathered = lax.all_gather(tokens, "row", axis=0, tiled=True)
    decode_cache = move_pages(prefill_cache, dest_col, dest_slot, pages_used)
    places, starts, ends = sorted_places(route_ids, gate_weight.shape[0])
    table = step_table(starts, ends, rows)
    partial_sums = up_products(table, places, gathered, gate_weight, up_weight)
    summed = lax.psum_scatter(partial_sums, "col", scatter_dimension=1, tiled=True).astype(jnp.float32)
    share = summed.shape[1]
    own_rows = lax.axis_index("col") * share + jnp.arange(share, dtype=jnp.int32)
    own_weight = jnp.sum(
        jnp.where(own_rows[:, None, None] == places[None], route_weight[None], 0.0), axis=(1, 2)
    )
    hidden = (own_weight[:, None] * jax.nn.silu(summed[0]) * summed[1]).astype(jnp.bfloat16)
    hidden_all = lax.all_gather(hidden, "col", axis=0, tiled=True)
    per_token = down_products(table, places, hidden_all, down_weight)
    mixed = lax.psum_scatter(per_token, "row", scatter_dimension=0, tiled=True)
    return (mixed, decode_cache)


def solution(mesh):
    in_specs = (
        P("row", "col"),
        P(None, "col", "row"),
        P(None, "col", "row"),
        P(None, "row", "col"),
        P(),
        P(),
        P(None, ("row", "col"), None, None),
        P("row", None, None),
        P("row", None, None),
        P("row", None),
    )
    out_specs = (P("row", "col"), P(None, ("row", "col"), None, None))
    return jax.shard_map(shards, mesh=mesh, in_specs=in_specs, out_specs=out_specs, check_vma=False)
```

```python
import jax
import jax.numpy as jnp
from jax import lax
from jax.experimental import pallas as pl
from jax.experimental.pallas import tpu as pltpu
from jax.sharding import PartitionSpec as P

TILE = 256
VMEM_BYTES = 48 * 1024 * 1024
CHUNKS = 2


def sorted_places(route_ids, experts):
    tokens = route_ids.shape[0]
    group = 128
    labels = jnp.arange(experts, dtype=jnp.int32)
    onehot = (route_ids[:, :, None] == labels).astype(jnp.float32)
    per_token = jnp.sum(onehot, axis=1).reshape(tokens // group, group, experts)
    below = jnp.tril(jnp.ones((group, group), jnp.bfloat16), -1)
    within = jnp.einsum(
        "ij,bje->bie", below, per_token.astype(jnp.bfloat16), preferred_element_type=jnp.float32
    )
    totals = jnp.sum(per_token, axis=1)
    blocks = jnp.arange(tokens // group)
    earlier = jnp.sum(jnp.where(blocks[:, None, None] > blocks[None, :, None], totals[None], 0.0), axis=1)
    counts = jnp.sum(totals, axis=0)
    starts = jnp.sum(jnp.where(labels[:, None] > labels[None, :], counts[None, :], 0.0), axis=1)
    base = (within + earlier[:, None, :] + starts).reshape(tokens, experts)
    places = jnp.sum(onehot * base[:, None, :], axis=2).astype(jnp.int32)
    starts = starts.astype(jnp.int32)
    return places, starts, starts + counts.astype(jnp.int32)


def step_table(starts, ends, rows):
    experts = starts.shape[0]
    tiles = rows // TILE
    labels = jnp.arange(experts, dtype=jnp.int32)
    spans = jnp.where(ends > starts, (ends - 1) // TILE - starts // TILE + 1, 0)
    after = jnp.sum(jnp.where(labels[:, None] >= labels[None, :], spans[None, :], 0), axis=1)
    step = jnp.arange(tiles + experts - 1, dtype=jnp.int32)
    expert = jnp.minimum(jnp.sum((after[None, :] <= step[:, None]).astype(jnp.int32), axis=1), experts - 1)
    chosen = expert[:, None] == labels[None, :]

    def pick(table):
        return jnp.sum(jnp.where(chosen, table[None, :], 0), axis=1)

    live = step < after[experts - 1]
    tile = jnp.where(live, pick(starts) // TILE + step - pick(after - spans), tiles - 1)
    low = jnp.where(live, jnp.maximum(pick(starts), tile * TILE), 0)
    high = jnp.where(live, jnp.minimum(pick(ends), tile * TILE + TILE), 0)
    return tile, expert, low, high


def up_kernel(tile, expert, low, high, first, second, tokens, gate, up, out):
    s = pl.program_id(0)

    @pl.when(high[s] > low[s])
    def _():
        place = tile[s] * TILE + lax.broadcasted_iota(jnp.int32, (TILE, 1), 0)
        mask = (place >= low[s]) & (place < high[s])
        pick = (first[...] == place) | (second[...] == place)
        rows = jnp.dot(
            jnp.where(pick, 1.0, 0.0).astype(jnp.bfloat16), tokens[...], preferred_element_type=jnp.float32
        ).astype(jnp.bfloat16)
        for i, weight in enumerate((gate, up)):
            product = jnp.dot(rows, weight[0], preferred_element_type=jnp.float32)
            out[i] = jnp.where(mask, product, out[i].astype(jnp.float32)).astype(jnp.bfloat16)


def up_products(table, places, tokens, gate_weight, up_weight):
    count = tokens.shape[0]
    rows = 2 * count // CHUNKS
    _, depth, width = gate_weight.shape
    whole = lambda s, *_: (0, 0)
    weight = pl.BlockSpec((1, depth, width), lambda s, tile, expert, *_: (expert[s], 0, 0))
    return pl.pallas_call(
        up_kernel,
        out_shape=jax.ShapeDtypeStruct((2, rows, width), jnp.bfloat16),
        grid_spec=pltpu.PrefetchScalarGridSpec(
            num_scalar_prefetch=4,
            grid=(table[0].shape[0],),
            in_specs=[
                pl.BlockSpec((1, count), whole),
                pl.BlockSpec((1, count), whole),
                pl.BlockSpec((count, depth), whole),
                weight,
                weight,
            ],
            out_specs=pl.BlockSpec((2, TILE, width), lambda s, tile, *_: (0, tile[s], 0)),
        ),
        compiler_params=pltpu.CompilerParams(vmem_limit_bytes=VMEM_BYTES),
        cost_estimate=pl.CostEstimate(
            flops=8 * rows * depth * width, bytes_accessed=2 * gate_weight.size * 2, transcendentals=0
        ),
    )(*table, places[:, 0].reshape(1, -1), places[:, 1].reshape(1, -1), tokens, gate_weight, up_weight)


def down_kernel(tile, expert, low, high, first, second, hidden, weight, total):
    s = pl.program_id(0)

    @pl.when(s == 0)
    def _():
        total[...] = jnp.zeros_like(total)

    @pl.when(high[s] > low[s])
    def _():
        place = tile[s] * TILE + lax.broadcasted_iota(jnp.int32, (1, TILE), 1)
        mask = (place >= low[s]) & (place < high[s])
        place = jnp.where(mask, place, -(1 << 30))
        pick = (first[...] == place) | (second[...] == place)
        product = jnp.dot(hidden[...], weight[0], preferred_element_type=jnp.float32).astype(jnp.bfloat16)
        total[...] += jnp.dot(
            jnp.where(pick, 1.0, 0.0).astype(jnp.bfloat16), product, preferred_element_type=jnp.float32
        )


def down_products(table, places, hidden, down_weight):
    count = places.shape[0]
    _, width, depth = down_weight.shape
    whole = lambda s, *_: (0, 0)
    return pl.pallas_call(
        down_kernel,
        out_shape=jax.ShapeDtypeStruct((count, depth), jnp.float32),
        grid_spec=pltpu.PrefetchScalarGridSpec(
            num_scalar_prefetch=4,
            grid=(table[0].shape[0],),
            in_specs=[
                pl.BlockSpec((count, 1), whole),
                pl.BlockSpec((count, 1), whole),
                pl.BlockSpec((TILE, width), lambda s, tile, *_: (tile[s], 0)),
                pl.BlockSpec((1, width, depth), lambda s, tile, expert, *_: (expert[s], 0, 0)),
            ],
            out_specs=pl.BlockSpec((count, depth), whole),
        ),
        compiler_params=pltpu.CompilerParams(vmem_limit_bytes=VMEM_BYTES),
        cost_estimate=pl.CostEstimate(
            flops=4 * hidden.size * depth, bytes_accessed=2 * down_weight.size, transcendentals=0
        ),
    )(*table, places[:, 0:1], places[:, 1:2], hidden, down_weight)


def page_kernel(source, keep, page, out):
    live = jnp.broadcast_to(keep[pl.program_id(0)] > 0, out.shape)
    out[...] = jnp.where(live, page[...], jnp.zeros_like(page))


def take_pages(cache, source, keep):
    block = (cache.shape[0], 1, *cache.shape[2:])
    return pl.pallas_call(
        page_kernel,
        out_shape=jax.ShapeDtypeStruct(cache.shape, cache.dtype),
        grid_spec=pltpu.PrefetchScalarGridSpec(
            num_scalar_prefetch=2,
            grid=(source.shape[0],),
            in_specs=[pl.BlockSpec(block, lambda p, source, keep: (0, source[p], 0, 0))],
            out_specs=pl.BlockSpec(block, lambda p, source, keep: (0, p, 0, 0)),
        ),
        cost_estimate=pl.CostEstimate(flops=0, bytes_accessed=8 * cache.size, transcendentals=0),
    )(source, keep, cache)


def move_pages(prefill_cache, dest_col, dest_slot, pages_used):
    col_devices = lax.axis_size("col")
    own = lax.axis_index("col")
    slots = prefill_cache.shape[1]
    per_peer = slots // col_devices
    page = jnp.arange(slots, dtype=jnp.int32)
    peers = jnp.arange(col_devices, dtype=jnp.int32)
    table = dest_col[0]
    earlier = (table[:, :, None] == table[:, None, :]) & (page[None, :] < page[:, None])[None]
    order = jnp.sum(earlier.astype(jnp.int32), axis=2)
    sends = table * per_peer + order
    is_own = (peers == own)[:, None]
    own_sends = jnp.sum(jnp.where(is_own, sends, 0), axis=0)
    own_used = jnp.sum(jnp.where(peers == own, pages_used[0], 0))
    source = jnp.sum(jnp.where(own_sends[None, :] == page[:, None], page[None, :], 0), axis=1)
    received = lax.all_to_all(
        take_pages(prefill_cache, source, (source < own_used).astype(jnp.int32)),
        "col",
        split_axis=1,
        concat_axis=1,
        tiled=True,
    )
    arrival = peers[:, None] * per_peer + order
    mine = (table == own)[None] & (dest_slot[0][None] == page[:, None, None])
    origin = jnp.sum(jnp.where(mine, arrival[None], 0), axis=(1, 2))
    return take_pages(received, origin, jnp.ones_like(origin))


def shards(
    tokens,
    gate_weight,
    up_weight,
    down_weight,
    route_ids,
    route_weight,
    prefill_cache,
    dest_col,
    dest_slot,
    pages_used,
):
    rows = 2 * route_ids.shape[0]
    gathered = lax.all_gather(tokens, "row", axis=0, tiled=True)
    decode_cache = move_pages(prefill_cache, dest_col, dest_slot, pages_used)
    places, starts, ends = sorted_places(route_ids, gate_weight.shape[0])
    span = rows // CHUNKS
    plans = []
    for chunk in range(CHUNKS):
        base = chunk * span
        table = step_table(jnp.clip(starts - base, 0, span), jnp.clip(ends - base, 0, span), span)
        plans.append((table, places - base))
    summed = [
        lax.psum_scatter(
            up_products(table, local, gathered, gate_weight, up_weight), "col", scatter_dimension=1, tiled=True
        )
        for table, local in plans
    ]
    share = span // lax.axis_size("col")
    own_rows = lax.axis_index("col") * share + jnp.arange(share, dtype=jnp.int32)
    hidden_all = []
    for (_, local), halves in zip(plans, summed):
        own_weight = jnp.sum(
            jnp.where(own_rows[:, None, None] == local[None], route_weight[None], 0.0), axis=(1, 2)
        )
        gate, up = halves[0].astype(jnp.float32), halves[1].astype(jnp.float32)
        hidden = (own_weight[:, None] * jax.nn.silu(gate) * up).astype(jnp.bfloat16)
        hidden_all.append(lax.all_gather(hidden, "col", axis=0, tiled=True))
    totals = [
        down_products(table, local, hidden, down_weight) for (table, local), hidden in zip(plans, hidden_all)
    ]
    per_token = sum(totals).astype(jnp.bfloat16)
    mixed = lax.psum_scatter(per_token, "row", scatter_dimension=0, tiled=True)
    return (mixed, decode_cache)


def solution(mesh):
    in_specs = (
        P("row", "col"),
        P(None, "col", "row"),
        P(None, "col", "row"),
        P(None, "row", "col"),
        P(),
        P(),
        P(None, ("row", "col"), None, None),
        P("row", None, None),
        P("row", None, None),
        P("row", None),
    )
    out_specs = (P("row", "col"), P(None, ("row", "col"), None, None))
    return jax.shard_map(shards, mesh=mesh, in_specs=in_specs, out_specs=out_specs, check_vma=False)
```
